32 devices in a mesh: row: 8 (over z, y), col: 4 (over x, core).
Axes of the slice: x: 2, y: 2, z: 4, core: 2. Of those that a mesh axis runs over, the one named last changes fastest.
Arguments:
- blocks: bfloat16 [512, 12, 128, 128], P('row'), may hold values from -0.15625 to 0.15625
- col_index: int32 [512, 12], P('row'), may hold values from -8 to 519, as said below
- live_slots: int32 [512], P('row'), may hold values from 3 to 12, as said below
- vectors: bfloat16 [256, 65536], P('col', 'row'), may hold values from -6 to 6
- center: float32 [1], replicated, may hold values from -0.4 to 0.4
- halfwidth: float32 [1], replicated, may hold values from 0.8 to 1.6
Outputs:
- ortho_basis: float32 [256, 65536], P('col', 'row')
- triangle: float32 [256, 256], replicated
The draws below stay inside these ranges and needn't reach their ends.
Inputs may be any that keep to these rules, and one draw needn't show every extreme that they name: col_index[i, k] - i lies in -8 .. 8 and is different for every k of a row; slot 0 is i, slot 1 is i + 8, slot 2 is i - 8. `live_slots`: slots 0, 1 and 2 are live in every row; the counts of one index of row lie within one of a level shared by that index (block rows 0 and 1 excepted), so whole devices are busy or light.
All inputs are finite; a program needn't handle non-finite values.
Results may differ from the reference program's by a relative error of at most 0.0042.
Values may be sent and summed in bfloat16 or wider, within the bound.
A program may use at most 128 MiB of HBM per device.

```python
import jax
import jax.numpy as jnp
from jax import lax

BLOCK = 128
NV = 256
K = 12
W = 8
BR_DEV = 64
NBR = 512
ORDER = 65536


def draw_col_index(key, part):
    row_ids = jnp.arange(NBR, dtype=jnp.int32)
    offsets_pool = jnp.concatenate([jnp.arange(-W + 1, 0, dtype=jnp.int32), jnp.arange(1, W, dtype=jnp.int32)])
    scores = jax.random.randint(jax.random.fold_in(key, 11), (NBR, 2 * W - 2), 0, 1 << 20) * (2 * W) + jnp.arange(2 * W - 2, dtype=jnp.int32)[None, :]
    ranking = jnp.argsort(scores, axis=1, stable=True)
    chosen = offsets_pool[ranking[:, :K - 3]]
    fixed_part = jnp.stack([jnp.zeros((NBR,), jnp.int32), jnp.full((NBR,), W, jnp.int32), jnp.full((NBR,), -W, jnp.int32)], axis=1)
    offsets_all = jnp.concatenate([fixed_part, chosen.astype(jnp.int32)], axis=1)
    return (row_ids[:, None] + offsets_all).astype(jnp.int32)


def draw_live_slots(key, part):
    groups = NBR // BR_DEV
    device_level = jax.random.randint(jax.random.fold_in(key, 21), (groups,), 3, K + 1)
    jitter = jax.random.randint(jax.random.fold_in(key, 22), (NBR,), -1, 2)
    counts = jnp.clip(jnp.repeat(device_level, BR_DEV) + jitter, 3, K)
    counts = counts.at[0].set(K).at[1].set(3)
    return counts.astype(jnp.int32)


def shard_levels(key, dims, pieces, smallest, high):
    level, own = 1.0, jax.random.fold_in(key, 6)
    for position, shards_of in pieces:
        draws = jnp.exp(jax.random.uniform(jax.random.fold_in(own, position), (shards_of,), jnp.float32, smallest / len(pieces), high / len(pieces)))
        level = level * jnp.repeat(draws, dims[position] // shards_of).reshape([-1 if axis == position else 1 for axis in range(len(dims))])
    return level


def noise(own_key, shape, spread, most, shards=(), held_as=jnp.bfloat16):
    factor_of = shard_levels(own_key, shape, shards, -0.22, 0.18) if shards else 1.0
    drawn = jax.random.normal(own_key, shape, jnp.float32) * spread * factor_of
    return jnp.minimum(jnp.maximum(drawn, -most), most).astype(held_as)


def setup_inputs(seed: int = 0) -> dict:
    arg_keys = jax.random.split(jax.random.key(seed), 7)
    return {
        "blocks": noise(arg_keys[0], (NBR, K, BLOCK, BLOCK), (BLOCK * K) ** -0.5, 0.15625, ((0, 8),)),
        "col_index": draw_col_index(jax.random.fold_in(arg_keys[6], 71), 0),
        "live_slots": draw_live_slots(jax.random.fold_in(arg_keys[6], 71), 0),
        "vectors": noise(arg_keys[3], (NV, ORDER), 1.0, 6.0, ((0, 4), (1, 8))),
        "center": jnp.clip(jax.random.uniform(arg_keys[4], (1,), jnp.float32, -0.4, 0.4), -0.4, 0.4),
        "halfwidth": jnp.clip(jax.random.uniform(arg_keys[5], (1,), jnp.float32, 0.8, 1.6), 0.8, 1.6),
    }


def apply_blocks(blocks, col_index, live_slots, vectors_in):
    extended = jnp.pad(vectors_in, ((0, 0), (W * BLOCK, W * BLOCK))).reshape(NV, NBR + 2 * W, BLOCK)
    groups = NBR // BR_DEV
    slot_live = jnp.arange(K, dtype=jnp.int32)[None, :] < live_slots[:, None]

    def group_product(packed):
        group_blocks, group_index, group_live = packed
        picked = jnp.take(extended, group_index.reshape(-1), axis=1).reshape(NV, BR_DEV, K, BLOCK)
        picked = jnp.where(group_live[None, :, :, None], picked.astype(jnp.float32), jnp.float32(0.0))
        return jnp.einsum('rkab,vrkb->vra', group_blocks.astype(jnp.float32), picked)
    products = lax.map(group_product, (blocks.reshape(groups, BR_DEV, K, BLOCK, BLOCK), (col_index + W).astype(jnp.int32).reshape(groups, BR_DEV, K), slot_live.reshape(groups, BR_DEV, K)))
    return jnp.transpose(products, (1, 0, 2, 3)).reshape(NV, ORDER)

def reference(blocks, col_index, live_slots, vectors, center, halfwidth):
    shift_value = center[0]
    scale_value = halfwidth[0]
    plain = vectors.astype(jnp.float32)
    first_step = ((apply_blocks(blocks, col_index, live_slots, vectors) - shift_value * plain) / scale_value).astype(jnp.bfloat16)
    second = apply_blocks(blocks, col_index, live_slots, first_step)
    filtered = (2.0 * (second - shift_value * first_step.astype(jnp.float32)) / scale_value - plain).astype(jnp.bfloat16)
    gram_matrix = lax.dot_general(filtered.astype(jnp.float32), filtered.astype(jnp.float32), (((1,), (1,)), ((), ())), preferred_element_type=jnp.float32) / ORDER
    factor = jnp.linalg.cholesky(gram_matrix)
    identity = jnp.eye(NV, dtype=gram_matrix.dtype)
    inverse = lax.linalg.triangular_solve(factor, identity, left_side=True, lower=True)
    ortho_basis = jnp.dot(inverse, filtered.astype(gram_matrix.dtype), precision=lax.Precision.HIGHEST)
    return (ortho_basis, factor.T)
```

```python
import functools

import jax
import jax.numpy as jnp
from jax import lax
from jax.experimental import pallas as pl
from jax.experimental.pallas import tpu as pltpu
from jax.sharding import PartitionSpec as P

W = 8
VMEM_BYTES = 56 * 1024 * 1024
NT = (((1,), (1,)), ((), ()))
TN = (((0,), (0,)), ((), ()))
NN = (((1,), (0,)), ((), ()))
HIGHEST = lax.Precision.HIGHEST


def halo(array, width):
    devices, length = lax.axis_size("row"), array.shape[1]
    up = [(i, (i + 1) % devices) for i in range(devices - 1)]
    down = [(j, i) for i, j in up]
    before = lax.ppermute(array[:, length - width :], "row", up)
    after = lax.ppermute(array[:, :width], "row", down)
    return before, after


def product_kernel(
    second, slots, per_step, index, live, shift, scale, blocks, before, field, after, *rest
):
    plain, out, extended = rest if second else (None, *rest)
    side = blocks.shape[2]
    step = pl.program_id(0)

    @pl.when(step == 0)
    def _():
        for i in range(W):
            extended[i] = before[:, i * side : (i + 1) * side]
            extended[extended.shape[0] - W + i] = after[:, i * side : (i + 1) * side]
        for i in range(extended.shape[0] - 2 * W):
            extended[W + i] = field[:, i * side : (i + 1) * side]

    inverse_scale = 1.0 / scale[0]
    for r in range(per_step):
        row = step * per_step + r
        count = live[row]
        picked = []
        for k in range(slots):
            value = extended[index[row * slots + k]]
            if k >= 3:
                value = jnp.where(k < count, value, jnp.zeros_like(value))
            picked.append(value)
        picked = jnp.concatenate(picked, axis=1)
        stored = jnp.concatenate([blocks[r, k] for k in range(slots)], axis=1)
        product = lax.dot_general(picked, stored, NT, preferred_element_type=jnp.float32)
        own = extended[W + row].astype(jnp.float32)
        value = (product - shift[0] * own) * inverse_scale
        if second:
            value = 2.0 * value - plain[:, r * side : (r + 1) * side].astype(jnp.float32)
        out[:, r * side : (r + 1) * side] = value.astype(out.dtype)


def product(blocks, index, live, shift, scale, field, plain=None):
    block_rows, slots, side, _ = blocks.shape
    width, length = field.shape
    before, after = halo(field, W * side)
    per_step = 4
    smem = pl.BlockSpec(memory_space=pltpu.SMEM)
    whole = pl.BlockSpec(memory_space=pltpu.VMEM)
    tile = pl.BlockSpec((width, per_step * side), lambda i: (0, i))
    second = plain is not None
    return pl.pallas_call(
        functools.partial(product_kernel, second, slots, per_step),
        grid=(block_rows // per_step,),
        out_shape=jax.ShapeDtypeStruct((width, length), jnp.bfloat16),
        in_specs=[smem] * 4
        + [pl.BlockSpec((per_step, slots, side, side), lambda i: (i, 0, 0, 0))]
        + [whole] * 3
        + ([tile] if second else []),
        out_specs=tile,
        scratch_shapes=[pltpu.VMEM((block_rows + 2 * W, width, side), jnp.bfloat16)],
        compiler_params=pltpu.CompilerParams(vmem_limit_bytes=VMEM_BYTES),
        cost_estimate=pl.CostEstimate(
            flops=2 * blocks.size * width, bytes_accessed=2 * blocks.size, transcendentals=0
        ),
    )(index, live, shift, scale, blocks, before, field, after, *([plain] if second else []))


def dot32(a, b, dims):
    return lax.dot_general(a, b, dims, precision=HIGHEST, preferred_element_type=jnp.float32)


def factor_block(matrix):
    n = matrix.shape[0]
    groups = [matrix[8 * g : 8 * g + 8] for g in range(n // 8)]
    lane = lax.broadcasted_iota(jnp.int32, (8, n), 1)
    sub = lax.broadcasted_iota(jnp.int32, (8, n), 0)
    upper = []
    for p in range(n // 8):
        panel = groups[p]
        saved = jnp.zeros_like(panel)
        for j in range(8):
            c = 8 * p + j
            column = jnp.broadcast_to(panel[:, c : c + 1], (8, n))
            pivot = jnp.broadcast_to(panel[j : j + 1, c : c + 1], (8, n))
            line = jnp.broadcast_to(panel[j : j + 1, :], (8, n))
            root = lax.rsqrt(pivot)
            line = line * root
            saved = jnp.where((sub == j) & (lane >= c), line, saved)
            line = jnp.where(lane == c, root, line)
            below = jnp.where(lane == c, 0.0, panel) - (column * root) * line
            panel = jnp.where(sub > j, below, jnp.where(sub == j, line, panel))
        upper.append(saved)
        inside = (lane >= 8 * p) & (lane < 8 * p + 8)
        panel = jnp.where(inside & (lane - 8 * p > sub), 0.0, panel)
        groups[p] = panel
        if p + 1 < n // 8:
            change = dot32(saved, panel, TN)
            for g in range(p + 1, n // 8):
                kept = jnp.where(inside, 0.0, groups[g])
                groups[g] = kept - change[8 * g : 8 * g + 8]
    row = lax.broadcasted_iota(jnp.int32, (n, n), 0)
    col = lax.broadcasted_iota(jnp.int32, (n, n), 1)
    inverse = jnp.where(row >= col, jnp.concatenate(groups, axis=0), 0.0)
    return jnp.concatenate(upper, axis=0), inverse


def finish_kernel(order, own_group, gram, field, basis, triangle, inverse):
    @pl.when(pl.program_id(0) == 0)
    def _():
        size = gram.shape[0]
        h = size // 2
        triangle[...] = jnp.zeros_like(triangle)
        inverse[...] = jnp.zeros_like(inverse)
        scaled = 1.0 / order
        u11, z11 = factor_block(gram[:h, :h] * scaled)
        u12 = dot32(z11, gram[:h, h:] * scaled, NN)
        u22, z22 = factor_block(gram[h:, h:] * scaled - dot32(u12, u12, TN))
        z21 = -dot32(z22, dot32(u12, z11, TN), NN)
        triangle[:h, :h] = u11
        triangle[:h, h:] = u12
        triangle[h:, h:] = u22
        inverse[:h, :h] = z11
        inverse[h:, :h] = z21
        inverse[h:, h:] = z22

    width = basis.shape[0]
    start = pl.multiple_of(own_group[0] * width, width)
    rows = inverse[pl.ds(start, width), :]
    high = rows.astype(jnp.bfloat16)
    left = rows - high.astype(jnp.float32)
    low = left.astype(jnp.bfloat16)
    rest = (left - low.astype(jnp.float32)).astype(jnp.bfloat16)
    both = jnp.concatenate([high, low, rest], axis=0)
    wide = jnp.dot(both, field[...], preferred_element_type=jnp.float32)
    basis[...] = wide[:width] + (wide[width : 2 * width] + wide[2 * width :])


def finish(gram, field, order, width):
    size, length = field.shape
    tile = min(length, 2048)
    group = lax.axis_index("col").astype(jnp.int32).reshape(1)
    whole = pl.BlockSpec((size, size), lambda i: (0, 0))
    return pl.pallas_call(
        functools.partial(finish_kernel, order),
        grid=(length // tile,),
        out_shape=(
            jax.ShapeDtypeStruct((width, length), jnp.float32),
            jax.ShapeDtypeStruct((size, size), jnp.float32),
        ),
        in_specs=[
            pl.BlockSpec(memory_space=pltpu.SMEM),
            whole,
            pl.BlockSpec((size, tile), lambda i: (0, i)),
        ],
        out_specs=(pl.BlockSpec((width, tile), lambda i: (0, i)), whole),
        scratch_shapes=[pltpu.VMEM((size, size), jnp.float32)],
        compiler_params=pltpu.CompilerParams(vmem_limit_bytes=VMEM_BYTES),
    )(group, gram, field)


def on_device(blocks, col_index, live_slots, vectors, center, halfwidth):
    block_rows = blocks.shape[0]
    order_all = vectors.shape[1] * lax.axis_size("row")
    index = (col_index - lax.axis_index("row") * block_rows + W).reshape(-1)
    first_step = product(blocks, index, live_slots, center, halfwidth, vectors)
    filtered = product(blocks, index, live_slots, center, halfwidth, first_step, vectors)
    all_columns = lax.all_gather(filtered, "col", axis=0, tiled=True)
    partial_gram = lax.dot_general(
        all_columns, all_columns, NT, preferred_element_type=jnp.float32
    )
    gram = lax.psum(partial_gram, "row")
    basis, triangle = finish(gram, all_columns, order_all, vectors.shape[0])
    return (basis, triangle)


def solution(mesh):
    in_specs = (P("row", None, None, None), P("row", None), P("row"), P("col", "row"), P(), P())
    out_specs = (P("col", "row"), P())
    return jax.shard_map(
        on_device, mesh=mesh, in_specs=in_specs, out_specs=out_specs, check_vma=False
    )
```

```python
import functools

import jax
import jax.numpy as jnp
from jax import lax
from jax.experimental import pallas as pl
from jax.experimental.pallas import tpu as pltpu
from jax.sharding import PartitionSpec as P

W = 8
VMEM_BYTES = 56 * 1024 * 1024
NT = (((1,), (1,)), ((), ()))
TN = (((0,), (0,)), ((), ()))
NN = (((1,), (0,)), ((), ()))
HIGHEST = lax.Precision.HIGHEST


def halo(array, width):
    devices, length = lax.axis_size("row"), array.shape[1]
    up = [(i, (i + 1) % devices) for i in range(devices - 1)]
    down = [(j, i) for i, j in up]
    before = lax.ppermute(array[:, length - width :], "row", up)
    after = lax.ppermute(array[:, :width], "row", down)
    return before, after


def product_kernel(
    second, slots, per_step, index, live, shift, scale, blocks, before, field, after, *rest
):
    plain, out, extended = rest if second else (None, *rest)
    side = blocks.shape[2]
    step = pl.program_id(0)

    @pl.when(step == 0)
    def _():
        for i in range(W):
            extended[i] = before[:, i * side : (i + 1) * side]
            extended[extended.shape[0] - W + i] = after[:, i * side : (i + 1) * side]
        for i in range(extended.shape[0] - 2 * W):
            extended[W + i] = field[:, i * side : (i + 1) * side]

    inverse_scale = 1.0 / scale[0]
    for r in range(per_step):
        row = step * per_step + r
        count = live[row]
        picked = []
        for k in range(slots):
            value = extended[index[row * slots + k]]
            if k >= 3:
                value = jnp.where(k < count, value, jnp.zeros_like(value))
            picked.append(value)
        picked = jnp.concatenate(picked, axis=1)
        stored = jnp.concatenate([blocks[r, k] for k in range(slots)], axis=1)
        product = lax.dot_general(picked, stored, NT, preferred_element_type=jnp.float32)
        own = extended[W + row].astype(jnp.float32)
        value = (product - shift[0] * own) * inverse_scale
        if second:
            value = 2.0 * value - plain[:, r * side : (r + 1) * side].astype(jnp.float32)
        out[:, r * side : (r + 1) * side] = value.astype(out.dtype)


def product(blocks, index, live, shift, scale, field, plain=None):
    block_rows, slots, side, _ = blocks.shape
    width, length = field.shape
    before, after = halo(field, W * side)
    per_step = 4
    smem = pl.BlockSpec(memory_space=pltpu.SMEM)
    whole = pl.BlockSpec(memory_space=pltpu.VMEM)
    tile = pl.BlockSpec((width, per_step * side), lambda i: (0, i))
    second = plain is not None
    return pl.pallas_call(
        functools.partial(product_kernel, second, slots, per_step),
        grid=(block_rows // per_step,),
        out_shape=jax.ShapeDtypeStruct((width, length), jnp.bfloat16),
        in_specs=[smem] * 4
        + [pl.BlockSpec((per_step, slots, side, side), lambda i: (i, 0, 0, 0))]
        + [whole] * 3
        + ([tile] if second else []),
        out_specs=tile,
        scratch_shapes=[pltpu.VMEM((block_rows + 2 * W, width, side), jnp.bfloat16)],
        compiler_params=pltpu.CompilerParams(vmem_limit_bytes=VMEM_BYTES),
        cost_estimate=pl.CostEstimate(
            flops=2 * blocks.size * width, bytes_accessed=2 * blocks.size, transcendentals=0
        ),
    )(index, live, shift, scale, blocks, before, field, after, *([plain] if second else []))


def dot32(a, b, dims):
    return lax.dot_general(a, b, dims, precision=HIGHEST, preferred_element_type=jnp.float32)


def factor_block(matrix):
    n = matrix.shape[0]
    groups = [matrix[8 * g : 8 * g + 8] for g in range(n // 8)]
    lane = lax.broadcasted_iota(jnp.int32, (8, n), 1)
    sub = lax.broadcasted_iota(jnp.int32, (8, n), 0)
    upper = []
    for p in range(n // 8):
        panel = groups[p]
        saved = jnp.zeros_like(panel)
        for j in range(8):
            c = 8 * p + j
            column = jnp.broadcast_to(panel[:, c : c + 1], (8, n))
            pivot = jnp.broadcast_to(panel[j : j + 1, c : c + 1], (8, n))
            line = jnp.broadcast_to(panel[j : j + 1, :], (8, n))
            root = lax.rsqrt(pivot)
            line = line * root
            saved = jnp.where((sub == j) & (lane >= c), line, saved)
            line = jnp.where(lane == c, root, line)
            below = jnp.where(lane == c, 0.0, panel) - (column * root) * line
            panel = jnp.where(sub > j, below, jnp.where(sub == j, line, panel))
        upper.append(saved)
        inside = (lane >= 8 * p) & (lane < 8 * p + 8)
        panel = jnp.where(inside & (lane - 8 * p > sub), 0.0, panel)
        groups[p] = panel
        if p + 1 < n // 8:
            change = dot32(saved, panel, TN)
            for g in range(p + 1, n // 8):
                kept = jnp.where(inside, 0.0, groups[g])
                groups[g] = kept - change[8 * g : 8 * g + 8]
    row = lax.broadcasted_iota(jnp.int32, (n, n), 0)
    col = lax.broadcasted_iota(jnp.int32, (n, n), 1)
    inverse = jnp.where(row >= col, jnp.concatenate(groups, axis=0), 0.0)
    return jnp.concatenate(upper, axis=0), inverse


def finish_kernel(order, own_group, gram, field, basis, triangle, inverse):
    @pl.when(pl.program_id(0) == 0)
    def _():
        size = gram.shape[0]
        h = size // 2
        triangle[...] = jnp.zeros_like(triangle)
        inverse[...] = jnp.zeros_like(inverse)
        scaled = 1.0 / order
        u11, z11 = factor_block(gram[:h, :h] * scaled)
        u12 = dot32(z11, gram[:h, h:] * scaled, NN)
        u22, z22 = factor_block(gram[h:, h:] * scaled - dot32(u12, u12, TN))
        z21 = -dot32(z22, dot32(u12, z11, TN), NN)
        triangle[:h, :h] = u11
        triangle[:h, h:] = u12
        triangle[h:, h:] = u22
        inverse[:h, :h] = z11
        inverse[h:, :h] = z21
        inverse[h:, h:] = z22

    width = basis.shape[0]
    start = pl.multiple_of(own_group[0] * width, width)
    rows = inverse[pl.ds(start, width), :]
    high = rows.astype(jnp.bfloat16)
    left = rows - high.astype(jnp.float32)
    low = left.astype(jnp.bfloat16)
    rest = (left - low.astype(jnp.float32)).astype(jnp.bfloat16)
    both = jnp.concatenate([high, low, rest], axis=0)
    wide = jnp.dot(both, field[...], preferred_element_type=jnp.float32)
    basis[...] = wide[:width] + (wide[width : 2 * width] + wide[2 * width :])


def finish(gram, field, order, width):
    size, length = field.shape
    tile = min(length, 2048)
    group = lax.axis_index("col").astype(jnp.int32).reshape(1)
    whole = pl.BlockSpec((size, size), lambda i: (0, 0))
    return pl.pallas_call(
        functools.partial(finish_kernel, order),
        grid=(length // tile,),
        out_shape=(
            jax.ShapeDtypeStruct((width, length), jnp.float32),
            jax.ShapeDtypeStruct((size, size), jnp.float32),
        ),
        in_specs=[
            pl.BlockSpec(memory_space=pltpu.SMEM),
            whole,
            pl.BlockSpec((size, tile), lambda i: (0, i)),
        ],
        out_specs=(pl.BlockSpec((width, tile), lambda i: (0, i)), whole),
        scratch_shapes=[pltpu.VMEM((size, size), jnp.float32)],
        compiler_params=pltpu.CompilerParams(vmem_limit_bytes=VMEM_BYTES),
    )(group, gram, field)


def gather_gram_kernel(own, everyone, gram, parts, inbox, gathered, chunk_send, chunk_recv, sems):
    rows, cols = lax.axis_size("row"), lax.axis_size("col")
    devices = rows * cols
    row, col = lax.axis_index("row"), lax.axis_index("col")
    me = row * cols + col
    width, length = own.shape
    chunk = length // cols

    def target(offset):
        flat = lax.rem(me + offset, devices)
        return {"row": lax.div(flat, cols), "col": lax.rem(flat, cols)}

    def flip(value, mask):
        for bit in bits:
            if mask & bit:
                value = value + bit * (1 - 2 * lax.rem(lax.div(value, bit), 2))
        return value

    bits = [1 << b for b in reversed(range(cols.bit_length() - 1))]
    barrier = pltpu.get_barrier_semaphore()

    def greet(offset, carry):
        pl.semaphore_signal(
            barrier, inc=1, device_id=target(offset), device_id_type=pl.DeviceIdType.MESH
        )
        return carry

    lax.fori_loop(1, devices, greet, 0)
    everyone[col] = own[...]
    pl.semaphore_wait(barrier, devices - 1)

    def piece(bit, mask, order):
        peer = flip(col, bit)
        place = pl.ds(pl.multiple_of(flip(peer, order) * chunk, 128), chunk)
        slot = slots[(bit, mask)] * cols + order
        view = everyone.at[flip(col, mask), :, place]
        return pltpu.make_async_remote_copy(
            src_ref=view,
            dst_ref=view,
            send_sem=chunk_send.at[slot],
            recv_sem=chunk_recv.at[slot],
            device_id={"row": row, "col": peer},
            device_id_type=pl.DeviceIdType.MESH,
        )

    slots, held, plan = {}, [0], []
    for bit in bits:
        for mask in held:
            slots[(bit, mask)] = len(slots)
            plan.append((bit, mask))
        held = held + [m ^ bit for m in held]
    waited = set()

    def arrived(bit, mask, order):
        if (bit, mask, order) not in waited:
            waited.add((bit, mask, order))
            piece(bit, mask, order).wait_recv()

    for order in range(cols):
        for bit in bits:
            piece(bit, 0, order).start()
    for order in range(cols):
        for bit, mask in plan:
            if mask:
                came = mask & -mask
                arrived(came, mask ^ came, bit ^ order)
                piece(bit, mask, order).start()
        if order == 0 or cols == 1:
            for bit, mask in plan:
                arrived(bit, mask, 0)
            share = everyone[:, :, pl.ds(pl.multiple_of(col * chunk, 128), chunk)]
            share = share.reshape(cols * width, chunk)
            partial = lax.dot_general(share, share, NT, preferred_element_type=jnp.float32)
            held_rows = parts.shape[1]
            for i in range(devices):
                parts[i] = partial[i * held_rows : (i + 1) * held_rows]

            def scatter(offset, carry):
                flat = lax.rem(me + offset, devices)
                pltpu.make_async_remote_copy(
                    src_ref=parts.at[flat],
                    dst_ref=inbox.at[offset - 1],
                    send_sem=sems.at[0],
                    recv_sem=sems.at[1],
                    device_id=target(offset),
                    device_id_type=pl.DeviceIdType.MESH,
                ).start()
                return carry

            lax.fori_loop(1, devices, scatter, 0)

    def settle(send, recv):
        return pltpu.make_async_remote_copy(
            src_ref=inbox,
            dst_ref=inbox,
            send_sem=sems.at[send],
            recv_sem=sems.at[recv],
            device_id=target(1),
            device_id_type=pl.DeviceIdType.MESH,
        )

    settle(0, 1).wait_recv()
    total = parts[me]
    for i in range(devices - 1):
        total = total + inbox[i]
    gathered[me] = total

    def spread(offset, carry):
        pltpu.make_async_remote_copy(
            src_ref=gathered.at[me],
            dst_ref=gathered.at[me],
            send_sem=sems.at[2],
            recv_sem=sems.at[3],
            device_id=target(offset),
            device_id_type=pl.DeviceIdType.MESH,
        ).start()
        return carry

    lax.fori_loop(1, devices, spread, 0)
    settle(2, 3).wait_recv()
    for i in range(devices):
        gram[i * parts.shape[1] : (i + 1) * parts.shape[1]] = gathered[i]
    for order in range(cols):
        for bit, mask in plan:
            arrived(bit, mask, order)
    for order in range(cols):
        for bit, mask in plan:
            piece(bit, mask, order).wait_send()
    settle(0, 1).wait_send()
    settle(2, 3).wait_send()


def gather_gram(own):
    cols = lax.axis_size("col")
    devices = cols * lax.axis_size("row")
    width, length = own.shape
    size = width * cols
    share = size // devices
    whole = pl.BlockSpec(memory_space=pltpu.VMEM)
    pieces = (cols - 1) * cols
    everyone, gram = pl.pallas_call(
        gather_gram_kernel,
        out_shape=(
            jax.ShapeDtypeStruct((cols, width, length), own.dtype),
            jax.ShapeDtypeStruct((size, size), jnp.float32),
        ),
        in_specs=[whole],
        out_specs=(whole, whole),
        scratch_shapes=[
            pltpu.VMEM((devices, share, size), jnp.float32),
            pltpu.VMEM((devices - 1, share, size), jnp.float32),
            pltpu.VMEM((devices, share, size), jnp.float32),
            pltpu.SemaphoreType.DMA((pieces,)),
            pltpu.SemaphoreType.DMA((pieces,)),
            pltpu.SemaphoreType.DMA((4,)),
        ],
        compiler_params=pltpu.CompilerParams(
            collective_id=0, has_side_effects=True, vmem_limit_bytes=VMEM_BYTES
        ),
    )(own)
    return everyone.reshape(size, length), gram


def on_device(blocks, col_index, live_slots, vectors, center, halfwidth):
    block_rows = blocks.shape[0]
    order_all = vectors.shape[1] * lax.axis_size("row")
    index = (col_index - lax.axis_index("row") * block_rows + W).reshape(-1)
    first_step = product(blocks, index, live_slots, center, halfwidth, vectors)
    filtered = product(blocks, index, live_slots, center, halfwidth, first_step, vectors)
    all_columns, gram = gather_gram(filtered)
    basis, triangle = finish(gram, all_columns, order_all, vectors.shape[0])
    return (basis, triangle)


def solution(mesh):
    in_specs = (P("row", None, None, None), P("row", None), P("row"), P("col", "row"), P(), P())
    out_specs = (P("col", "row"), P())
    return jax.shard_map(
        on_device, mesh=mesh, in_specs=in_specs, out_specs=out_specs, check_vma=False
    )
```

```python
import functools

import jax
import jax.numpy as jnp
from jax import lax
from jax.experimental import pallas as pl
from jax.experimental.pallas import tpu as pltpu
from jax.sharding import PartitionSpec as P

W = 8
VMEM_BYTES = 56 * 1024 * 1024
NT = (((1,), (1,)), ((), ()))
TN = (((0,), (0,)), ((), ()))
NN = (((1,), (0,)), ((), ()))
HIGHEST = lax.Precision.HIGHEST


def halo(array, width):
    devices, length = lax.axis_size("row"), array.shape[1]
    up = [(i, (i + 1) % devices) for i in range(devices - 1)]
    down = [(j, i) for i, j in up]
    before = lax.ppermute(array[:, length - width :], "row", up)
    after = lax.ppermute(array[:, :width], "row", down)
    return before, after


def product_kernel(
    second, slots, per_step, index, live, shift, scale, blocks, before, field, after, *rest
):
    plain, out, extended = rest if second else (None, *rest)
    side = blocks.shape[2]
    step = pl.program_id(0)

    @pl.when(step == 0)
    def _():
        for i in range(W):
            extended[i] = before[:, i * side : (i + 1) * side]
            extended[extended.shape[0] - W + i] = after[:, i * side : (i + 1) * side]
        for i in range(extended.shape[0] - 2 * W):
            extended[W + i] = field[:, i * side : (i + 1) * side]

    inverse_scale = 1.0 / scale[0]
    for r in range(per_step):
        row = step * per_step + r
        count = live[row]
        picked = []
        for k in range(slots):
            value = extended[index[row * slots + k]]
            if k >= 3:
                value = jnp.where(k < count, value, jnp.zeros_like(value))
            picked.append(value)
        picked = jnp.concatenate(picked, axis=1)
        stored = jnp.concatenate([blocks[r, k] for k in range(slots)], axis=1)
        product = lax.dot_general(stored, picked, NT, preferred_element_type=jnp.float32).T
        own = extended[W + row].astype(jnp.float32)
        value = (product - shift[0] * own) * inverse_scale
        if second:
            value = 2.0 * value - plain[:, r * side : (r + 1) * side].astype(jnp.float32)
        out[:, r * side : (r + 1) * side] = value.astype(out.dtype)


def product(blocks, index, live, shift, scale, field, plain=None):
    block_rows, slots, side, _ = blocks.shape
    width, length = field.shape
    before, after = halo(field, W * side)
    per_step = 8
    smem = pl.BlockSpec(memory_space=pltpu.SMEM)
    whole = pl.BlockSpec(memory_space=pltpu.VMEM)
    tile = pl.BlockSpec((width, per_step * side), lambda i: (0, i))
    second = plain is not None
    return pl.pallas_call(
        functools.partial(product_kernel, second, slots, per_step),
        grid=(block_rows // per_step,),
        out_shape=jax.ShapeDtypeStruct((width, length), jnp.bfloat16),
        in_specs=[smem] * 4
        + [pl.BlockSpec((per_step, slots, side, side), lambda i: (i, 0, 0, 0))]
        + [whole] * 3
        + ([tile] if second else []),
        out_specs=tile,
        scratch_shapes=[pltpu.VMEM((block_rows + 2 * W, width, side), jnp.bfloat16)],
        compiler_params=pltpu.CompilerParams(vmem_limit_bytes=VMEM_BYTES),
        cost_estimate=pl.CostEstimate(
            flops=2 * blocks.size * width, bytes_accessed=2 * blocks.size, transcendentals=0
        ),
    )(index, live, shift, scale, blocks, before, field, after, *([plain] if second else []))


def dot32(a, b, dims):
    return lax.dot_general(a, b, dims, precision=HIGHEST, preferred_element_type=jnp.float32)


def factor_block(matrix):
    n = matrix.shape[0]
    groups = [matrix[8 * g : 8 * g + 8] for g in range(n // 8)]
    lane = lax.broadcasted_iota(jnp.int32, (8, n), 1)
    sub = lax.broadcasted_iota(jnp.int32, (8, n), 0)
    upper = []

    def spread_row(value, j):
        return jnp.broadcast_to(value[j : j + 1, :], (8, n))

    def spread_columns(value, p):
        return [
            jnp.broadcast_to(value[:, 8 * p + m : 8 * p + m + 1], (8, n)) for m in range(8)
        ]

    for p in range(n // 8):
        panel = groups[p]
        columns = spread_columns(panel, p)
        saved = jnp.zeros_like(panel)
        roots, factors = [], []
        for j in range(8):
            c = 8 * p + j
            root = lax.rsqrt(spread_row(columns[j], j))
            scaled = columns[j] * root
            across = [spread_row(scaled, m) for m in range(j + 1, 8)]
            for m in range(j + 1, 8):
                columns[m] = columns[m] - scaled * across[m - j - 1]
            roots.append(root)
            factors.append(across)
            line = spread_row(panel, j) * root
            saved = jnp.where((sub == j) & (lane >= c), line, saved)
            line = jnp.where(lane == c, root, line)
            below = jnp.where(lane == c, 0.0, panel) - scaled * line
            panel = jnp.where(sub > j, below, jnp.where(sub == j, line, panel))
        upper.append(saved)
        inside = (lane >= 8 * p) & (lane < 8 * p + 8)
        panel = jnp.where(inside & (lane - 8 * p > sub), 0.0, panel)
        groups[p] = panel
        lines = [spread_row(panel, j) for j in range(8)]
        for g in range(p + 1, n // 8):
            columns = spread_columns(groups[g], p)
            rest = jnp.where(inside, 0.0, groups[g])
            for j in range(8):
                scaled = columns[j] * roots[j]
                for m in range(j + 1, 8):
                    columns[m] = columns[m] - scaled * factors[j][m - j - 1]
                rest = rest - scaled * lines[j]
            groups[g] = rest
    row = lax.broadcasted_iota(jnp.int32, (n, n), 0)
    col = lax.broadcasted_iota(jnp.int32, (n, n), 1)
    inverse = jnp.where(row >= col, jnp.concatenate(groups, axis=0), 0.0)
    return jnp.concatenate(upper, axis=0), inverse


def finish_kernel(order, own_group, gram, field, basis, triangle, inverse):
    @pl.when(pl.program_id(0) == 0)
    def _():
        size = gram.shape[0]
        h = size // 2
        triangle[...] = jnp.zeros_like(triangle)
        inverse[...] = jnp.zeros_like(inverse)
        scaled = 1.0 / order
        u11, z11 = factor_block(gram[:h, :h] * scaled)
        u12 = dot32(z11, gram[:h, h:] * scaled, NN)
        u22, z22 = factor_block(gram[h:, h:] * scaled - dot32(u12, u12, TN))
        z21 = -dot32(z22, dot32(u12, z11, TN), NN)
        triangle[:h, :h] = u11
        triangle[:h, h:] = u12
        triangle[h:, h:] = u22
        inverse[:h, :h] = z11
        inverse[h:, :h] = z21
        inverse[h:, h:] = z22

    width = basis.shape[0]
    start = pl.multiple_of(own_group[0] * width, width)
    rows = inverse[pl.ds(start, width), :]
    high = rows.astype(jnp.bfloat16)
    left = rows - high.astype(jnp.float32)
    low = left.astype(jnp.bfloat16)
    rest = (left - low.astype(jnp.float32)).astype(jnp.bfloat16)
    both = jnp.concatenate([high, low, rest], axis=0)
    wide = jnp.dot(both, field[...], preferred_element_type=jnp.float32)
    basis[...] = wide[:width] + (wide[width : 2 * width] + wide[2 * width :])


def finish(gram, field, order, width):
    size, length = field.shape
    tile = min(length, 2048)
    group = lax.axis_index("col").astype(jnp.int32).reshape(1)
    whole = pl.BlockSpec((size, size), lambda i: (0, 0))
    return pl.pallas_call(
        functools.partial(finish_kernel, order),
        grid=(length // tile,),
        out_shape=(
            jax.ShapeDtypeStruct((width, length), jnp.float32),
            jax.ShapeDtypeStruct((size, size), jnp.float32),
        ),
        in_specs=[
            pl.BlockSpec(memory_space=pltpu.SMEM),
            whole,
            pl.BlockSpec((size, tile), lambda i: (0, i)),
        ],
        out_specs=(pl.BlockSpec((width, tile), lambda i: (0, i)), whole),
        scratch_shapes=[pltpu.VMEM((size, size), jnp.float32)],
        compiler_params=pltpu.CompilerParams(vmem_limit_bytes=VMEM_BYTES),
    )(group, gram, field)


def gather_gram_kernel(own, everyone, gram, parts, inbox, gathered, chunk_send, chunk_recv, sems):
    rows, cols = lax.axis_size("row"), lax.axis_size("col")
    devices = rows * cols
    row, col = lax.axis_index("row"), lax.axis_index("col")
    me = row * cols + col
    width, length = own.shape
    chunk = length // cols

    def target(offset):
        flat = lax.rem(me + offset, devices)
        return {"row": lax.div(flat, cols), "col": lax.rem(flat, cols)}

    def flip(value, mask):
        for bit in bits:
            if mask & bit:
                value = value + bit * (1 - 2 * lax.rem(lax.div(value, bit), 2))
        return value

    bits = [1 << b for b in reversed(range(cols.bit_length() - 1))]
    barrier = pltpu.get_barrier_semaphore()

    def greet(offset, carry):
        pl.semaphore_signal(
            barrier, inc=1, device_id=target(offset), device_id_type=pl.DeviceIdType.MESH
        )
        return carry

    lax.fori_loop(1, devices, greet, 0)
    everyone[col] = own[...]
    pl.semaphore_wait(barrier, devices - 1)

    def piece(bit, mask, order):
        peer = flip(col, bit)
        place = pl.ds(pl.multiple_of(flip(peer, order) * chunk, 128), chunk)
        slot = slots[(bit, mask)] * cols + order
        view = everyone.at[flip(col, mask), :, place]
        return pltpu.make_async_remote_copy(
            src_ref=view,
            dst_ref=view,
            send_sem=chunk_send.at[slot],
            recv_sem=chunk_recv.at[slot],
            device_id={"row": row, "col": peer},
            device_id_type=pl.DeviceIdType.MESH,
        )

    slots, held, plan = {}, [0], []
    for bit in bits:
        for mask in held:
            slots[(bit, mask)] = len(slots)
            plan.append((bit, mask))
        held = held + [m ^ bit for m in held]
    waited = set()

    def arrived(bit, mask, order):
        if (bit, mask, order) not in waited:
            waited.add((bit, mask, order))
            piece(bit, mask, order).wait_recv()

    def launch(orders):
        for order in orders:
            for bit, mask in plan:
                if mask == 0:
                    piece(bit, mask, order).start()

    def forward(orders):
        for order in orders:
            for bit, mask in plan:
                if mask:
                    came = mask & -mask
                    arrived(came, mask ^ came, bit ^ order)
                    piece(bit, mask, order).start()

    early = (cols + 1) // 2
    launch(range(early))
    forward(range(early))
    for bit, mask in plan:
        arrived(bit, mask, 0)
    share = everyone[:, :, pl.ds(pl.multiple_of(col * chunk, 128), chunk)]
    share = share.reshape(cols * width, chunk)
    partial = lax.dot_general(share, share, NT, preferred_element_type=jnp.float32)
    held_rows = parts.shape[1]
    for i in range(devices):
        parts[i] = partial[i * held_rows : (i + 1) * held_rows]

    def scatter(offset, carry):
        flat = lax.rem(me + offset, devices)
        pltpu.make_async_remote_copy(
            src_ref=parts.at[flat],
            dst_ref=inbox.at[offset - 1],
            send_sem=sems.at[0],
            recv_sem=sems.at[1],
            device_id=target(offset),
            device_id_type=pl.DeviceIdType.MESH,
        ).start()
        return carry

    lax.fori_loop(1, devices, scatter, 0)
    launch(range(early, cols))

    def settle(send, recv):
        return pltpu.make_async_remote_copy(
            src_ref=inbox,
            dst_ref=inbox,
            send_sem=sems.at[send],
            recv_sem=sems.at[recv],
            device_id=target(1),
            device_id_type=pl.DeviceIdType.MESH,
        )

    settle(0, 1).wait_recv()
    total = parts[me]
    for i in range(devices - 1):
        total = total + inbox[i]
    gathered[me] = total

    def spread(offset, carry):
        pltpu.make_async_remote_copy(
            src_ref=gathered.at[me],
            dst_ref=gathered.at[me],
            send_sem=sems.at[2],
            recv_sem=sems.at[3],
            device_id=target(offset),
            device_id_type=pl.DeviceIdType.MESH,
        ).start()
        return carry

    lax.fori_loop(1, devices, spread, 0)
    forward(range(early, cols))
    settle(2, 3).wait_recv()
    for i in range(devices):
        gram[i * parts.shape[1] : (i + 1) * parts.shape[1]] = gathered[i]
    for order in range(cols):
        for bit, mask in plan:
            arrived(bit, mask, order)
    for order in range(cols):
        for bit, mask in plan:
            piece(bit, mask, order).wait_send()
    settle(0, 1).wait_send()
    settle(2, 3).wait_send()


def gather_gram(own):
    cols = lax.axis_size("col")
    devices = cols * lax.axis_size("row")
    width, length = own.shape
    size = width * cols
    share = size // devices
    whole = pl.BlockSpec(memory_space=pltpu.VMEM)
    pieces = (cols - 1) * cols
    everyone, gram = pl.pallas_call(
        gather_gram_kernel,
        out_shape=(
            jax.ShapeDtypeStruct((cols, width, length), own.dtype),
            jax.ShapeDtypeStruct((size, size), jnp.float32),
        ),
        in_specs=[whole],
        out_specs=(whole, whole),
        scratch_shapes=[
            pltpu.VMEM((devices, share, size), jnp.float32),
            pltpu.VMEM((devices - 1, share, size), jnp.float32),
            pltpu.VMEM((devices, share, size), jnp.float32),
            pltpu.SemaphoreType.DMA((pieces,)),
            pltpu.SemaphoreType.DMA((pieces,)),
            pltpu.SemaphoreType.DMA((4,)),
        ],
        compiler_params=pltpu.CompilerParams(
            collective_id=0, has_side_effects=True, vmem_limit_bytes=VMEM_BYTES
        ),
    )(own)
    return everyone.reshape(size, length), gram


def on_device(blocks, col_index, live_slots, vectors, center, halfwidth):
    block_rows = blocks.shape[0]
    order_all = vectors.shape[1] * lax.axis_size("row")
    index = (col_index - lax.axis_index("row") * block_rows + W).reshape(-1)
    first_step = product(blocks, index, live_slots, center, halfwidth, vectors)
    filtered = product(blocks, index, live_slots, center, halfwidth, first_step, vectors)
    all_columns, gram = gather_gram(filtered)
    basis, triangle = finish(gram, all_columns, order_all, vectors.shape[0])
    return (basis, triangle)


def solution(mesh):
    in_specs = (P("row", None, None, None), P("row", None), P("row"), P("col", "row"), P(), P())
    out_specs = (P("col", "row"), P())
    return jax.shard_map(
        on_device, mesh=mesh, in_specs=in_specs, out_specs=out_specs, check_vma=False
    )
```
